32 devices in a mesh: groups: 2 (over y), row: 4 (over x, core), col: 4 (over z).
Axes of the slice: x: 2, y: 2, z: 4, core: 2. Of those that a mesh axis runs over, the one named last changes fastest.
Arguments:
- tokens: float32 [512, 16384], P(('groups', 'col'), 'row'), parts along dimension 0, may hold values from -6 to 6
- weight: float32 [16384, 16384], P('row', 'col'), may hold values from -0.046875 to 0.046875
- token_amax: float32 [8, 4, 16], P('groups', 'row'), parts along dimension 0, may hold values from 0.25 to 3
- token_window: int32 [8, 4], P('groups', 'row'), parts along dimension 0, may hold values from 1 to 16
- weight_amax: float32 [4, 4, 16], P('row', 'col'), may hold values from 0.002 to 0.025
- weight_window: int32 [4, 4], P('row', 'col'), may hold values from 1 to 16
Outputs:
- projected: bfloat16 [512, 16384], P(('groups', 'row'), 'col'), parts along dimension 0
The draws below stay inside these ranges and needn't reach their ends.
There are 2 independent parts, one for each index of `groups`. The reference program is written for one: setup_inputs(seed, part) draws one part's arguments, and reference() takes and returns one part's arrays. A program takes and returns all parts, laid end to end along the dimension named above; an argument that names none is the same for every part. Nothing has to cross between parts.
Inputs may be any that keep to these rules, and one draw needn't show every extreme that they name: `token_window`: the number of newest history entries that a block's scale uses. `weight_window`: the number of newest history entries that a tile's scale uses.
All inputs are finite; a program needn't handle non-finite values.
Results may differ from the reference program's by a relative error of at most 0.0056.
Values may be sent and summed in bfloat16 or wider, within the bound.
A program may use at most 192 MiB of HBM per device.

```python
import math
import jax
import jax.numpy as jnp

D_IN = 16384
D_OUT = 16384
TOK_DEV = 64
HIST = 16
TOKENS = 256
N_ROW = 4
N_COL = 4


def touch_ends(entries, key, low, largest):
    place = [jax.random.randint(jax.random.fold_in(key, axis), (), 0, length) for axis, length in enumerate(entries.shape)]
    main_axis = entries.shape.index(max(entries.shape))
    next_to = place[:main_axis] + [(place[main_axis] + 1) % entries.shape[main_axis]] + place[main_axis + 1:]
    return entries.at[tuple(place)].set(low).at[tuple(next_to)].set(largest)


def block_scale(rng, shape, pieces, smallest, top_value):
    factor_of, own = 1.0, jax.random.fold_in(rng, 6)
    for dim, shards_of in pieces:
        steps = jnp.exp(jax.random.uniform(jax.random.fold_in(own, dim), (shards_of,), jnp.float32, smallest / len(pieces), top_value / len(pieces)))
        factor_of = factor_of * jnp.repeat(steps, shape[dim] // shards_of).reshape([-1 if axis == dim else 1 for axis in range(len(shape))])
    return factor_of


def gaussian(own_key, dims, scale, limit, cuts=(), kind=jnp.bfloat16):
    entries = jax.random.normal(own_key, dims, jnp.float32) * scale
    if len(cuts) > 0:
        entries = block_scale(own_key, dims, cuts, -0.22, 0.18) * entries
    return jnp.clip(entries, min=-limit, max=limit).astype(kind)


def setup_inputs(seed: int = 0, part: int = 0) -> dict:
    key_list = jax.random.split(jax.random.key(seed), 7)
    own_keys = jax.random.split(jax.random.fold_in(key_list[6], part), 7)
    return {
        "tokens": gaussian(own_keys[0], (TOKENS, D_IN), 1.0, 6.0, ((0, 4), (1, 4)), jnp.float32),
        "weight": gaussian(key_list[1], (D_IN, D_OUT), D_IN ** -0.5, 0.046875, ((0, 4), (1, 4)), jnp.float32),
        "token_amax": jnp.clip(jnp.exp(math.log(3.0) - 2.4849066 * jax.random.uniform(own_keys[2], (N_COL, N_ROW, HIST), jnp.float32) ** block_scale(own_keys[2], (N_COL, N_ROW, HIST), ((1, 4),), -0.2, 0.2)), 0.25, 3.0),
        "token_window": touch_ends(jax.random.randint(own_keys[3], (N_COL, N_ROW), 1, HIST + 1), jax.random.fold_in(own_keys[3], 1), 1, HIST).astype(jnp.int32),
        "weight_amax": jnp.clip(jnp.exp(math.log(0.025) - 2.5257286 * jax.random.uniform(key_list[4], (N_ROW, N_COL, HIST), jnp.float32) ** block_scale(key_list[4], (N_ROW, N_COL, HIST), ((0, 4), (1, 4)), -0.2, 0.2)), 0.002, 0.025),
        "weight_window": touch_ends(jax.random.randint(key_list[5], (N_ROW, N_COL), 1, HIST + 1), jax.random.fold_in(key_list[5], 1), 1, HIST).astype(jnp.int32),
    }


QMAX = 448.0


def delayed_scale(history, window):
    hlen = history.shape[-1]
    position = jnp.arange(hlen, dtype=jnp.int32)
    keep = position >= (hlen - window)[..., None]
    amax = jnp.max(jnp.where(keep, history, jnp.float32(0.0)), axis=-1)
    return QMAX / amax


def quantize(values, scale):
    return jnp.clip(values * scale, -QMAX, QMAX).astype(jnp.bfloat16)


def reference(tokens, weight, token_amax, token_window, weight_amax, weight_window):
    token_scale = delayed_scale(token_amax, token_window)
    weight_scale = delayed_scale(weight_amax, weight_window)
    in_dev = D_IN // N_ROW
    out_dev = D_OUT // N_COL
    blocked = tokens.reshape(N_COL, TOK_DEV, N_ROW, in_dev)
    token_q = quantize(blocked, token_scale[:, None, :, None]).reshape(TOKENS, D_IN)
    tiles = weight.reshape(N_ROW, in_dev, N_COL, out_dev)
    weight_q = quantize(tiles, weight_scale[:, None, :, None]).reshape(D_IN, D_OUT)
    total = jnp.zeros((TOKENS, D_OUT), jnp.float32)
    for index in range(N_ROW):
        lo = index * in_dev
        partial_sum = jnp.dot(token_q[:, lo:lo + in_dev], weight_q[lo:lo + in_dev, :], preferred_element_type=jnp.float32)
        descale = 1.0 / (token_scale[:, index][:, None] * weight_scale[index][None, :])
        spread = jnp.repeat(jnp.repeat(descale, TOK_DEV, axis=0), out_dev, axis=1)
        total = total + partial_sum * spread
    return total.astype(jnp.bfloat16)
```

```python
import functools

import jax
import jax.numpy as jnp
from jax import lax
from jax.experimental import pallas as pl
from jax.experimental.pallas import tpu as pltpu
from jax.sharding import PartitionSpec as P

TOK_DEV = 64
QMAX = 448.0
MESH = pl.DeviceIdType.MESH
MIB = 1 << 20


def delayed_scale(history, window):
    hlen = history.shape[-1]
    position = jnp.arange(hlen, dtype=jnp.int32)
    keep = position >= (hlen - window)[..., None]
    amax = jnp.max(jnp.where(keep, history, jnp.float32(0.0)), axis=-1)
    return QMAX / amax


def quantize(values, scale):
    return jnp.clip(values * scale, -QMAX, QMAX).astype(jnp.bfloat16)


def row_descale(table, count):
    block_of = jnp.arange(count, dtype=jnp.int32) // TOK_DEV
    owners = jnp.arange(table.shape[0], dtype=jnp.int32)
    onehot = block_of[:, None] == owners[None, :]
    return jnp.sum(jnp.where(onehot, table[None, :], jnp.float32(0.0)), axis=1)


def general(tokens, weight, token_amax, token_window, weight_amax, weight_window):
    token_scale = delayed_scale(token_amax[:, 0, :], token_window[:, 0])
    own_scale = lax.dynamic_index_in_dim(token_scale, lax.axis_index("col"), 0, keepdims=False)
    tile_scale = delayed_scale(weight_amax[0, 0, :], weight_window[0, 0])
    token_q = quantize(tokens, own_scale)
    weight_q = quantize(weight, tile_scale)
    table = 1.0 / (token_scale * tile_scale)
    piece = lax.all_gather(token_q, "col", axis=0, tiled=True)
    values = jnp.dot(piece, weight_q, preferred_element_type=jnp.float32)
    partial_sum = values * row_descale(table, piece.shape[0])[:, None]
    summed = lax.psum_scatter(partial_sum, "row", scatter_dimension=0, tiled=True)
    return summed.astype(jnp.bfloat16)


def window_scale(history, window):
    position = lax.broadcasted_iota(jnp.int32, history.shape, 1)
    keep = position >= history.shape[1] - window
    return QMAX / jnp.max(jnp.where(keep, history, 0.0), axis=1, keepdims=True)


def fused(dims, tok_hbm, w_hbm, tam, twin, wam, wwin, out,
          tokf, stage, wq, tq, mine, psend, prec, xsend, xrec, accb,
          tok_sem, stage_sem, zs, zr, ps, pr, xs, xr):
    rows, depth, wide, nstage = dims
    half, dk = rows // 2, depth // 2
    groups = wq.shape[0]
    z, r = lax.axis_index("col"), lax.axis_index("row")
    x, c = r // 2, r % 2
    sibling, across = x * 2 + (1 - c), (1 - x) * 2 + c
    middle = (z % 3) != 0

    low = z < 2
    zz = jnp.where(low, z, 3 - z)

    def order(k):
        b = (k + zz) % 2 if k < 2 else k
        return jnp.where(low, b, 3 - b)

    blocks = [order(k) for k in range(4)]

    def stage_copy(g, kk, slot):
        return pltpu.make_async_copy(
            w_hbm.at[pl.ds(kk * dk, dk), pl.ds(pl.multiple_of(g * wide, wide), wide)],
            stage.at[slot], stage_sem.at[slot])

    tok_copy = pltpu.make_async_copy(tok_hbm, tokf, tok_sem)
    tok_copy.start()
    for i in range(nstage):
        stage_copy(i // 2, i % 2, i).start()

    barrier = pltpu.get_barrier_semaphore()
    for who in (sibling, across):
        pl.semaphore_signal(barrier, inc=1, device_id={"row": who}, device_id_type=MESH)

    @pl.when(z > 0)
    def _():
        pl.semaphore_signal(barrier, inc=1, device_id={"col": z - 1}, device_id_type=MESH)

    @pl.when(z < 3)
    def _():
        pl.semaphore_signal(barrier, inc=1, device_id={"col": z + 1}, device_id_type=MESH)

    token_scale = window_scale(tam[:, 0, :], twin[...])
    weight_scale = window_scale(wam[0], wwin[...])
    table = 1.0 / (token_scale * weight_scale)
    which = lax.broadcasted_iota(jnp.int32, table.shape, 0)

    def pick(values, b):
        return jnp.sum(jnp.where(which == b, values, 0.0), axis=0, keepdims=True)

    own_scale = pick(token_scale, z)

    def z_copy(b, p, right):
        to = z + 1 if right else z - 1
        piece = b * 4 + p
        return pltpu.make_async_remote_copy(
            src_ref=tq.at[piece], dst_ref=tq.at[piece],
            send_sem=zs.at[int(right) * 16 + piece], recv_sem=zr.at[piece],
            device_id={"col": to}, device_id_type=MESH)

    def hop(b, p, act):
        @pl.when(b > z)
        def _():
            act(z_copy(b, p, False))

        @pl.when(b < z)
        def _():
            act(z_copy(b, p, True))

    def forward(b, p):
        @pl.when(middle)
        def _():
            z_copy(b, p, True).wait_recv()
            hop(b, p, lambda copy: copy.start())

    def arrive(b, p):
        @pl.when(jnp.logical_not(middle))
        def _():
            z_copy(b, p, True).wait_recv()

    def p_copy(slot, h, g):
        unit = (slot * 2 + h) * groups + g
        return pltpu.make_async_remote_copy(
            src_ref=psend.at[unit], dst_ref=prec.at[unit],
            send_sem=ps.at[unit], recv_sem=pr.at[unit],
            device_id={"row": sibling}, device_id_type=MESH)

    def x_copy(h, g):
        unit = h * groups + g
        return pltpu.make_async_remote_copy(
            src_ref=xsend.at[unit], dst_ref=xrec.at[unit],
            send_sem=xs.at[unit], recv_sem=xr.at[unit],
            device_id={"row": across}, device_id_type=MESH)

    def give(b, h, g, values):
        slot = (b // 2 + x) % 2
        unit = (slot * 2 + h) * groups + g

        @pl.when(b % 2 != c)
        def _():
            psend[unit] = values.astype(jnp.bfloat16)
            p_copy(slot, h, g).start()

        @pl.when(b % 2 == c)
        def _():
            mine[unit] = values

    def pair_sum(b, h, g):
        slot = (b // 2 + x) % 2
        unit = (slot * 2 + h) * groups + g

        @pl.when(b % 2 == c)
        def _():
            p_copy(slot, h, g).wait_recv()
            total = mine[unit] + prec[unit].astype(jnp.float32)

            @pl.when(slot == 1)
            def _():
                xsend[h * groups + g] = total.astype(jnp.bfloat16)
                x_copy(h, g).start()

            @pl.when(slot == 0)
            def _():
                mine[unit] = total

    def final_sum(h, g):
        unit = h * groups + g
        x_copy(h, g).wait_recv()
        total = mine[unit] + xrec[unit].astype(jnp.float32)
        out[pl.ds(h * half, half), pl.ds(pl.multiple_of(g * wide, wide), wide)] = total.astype(jnp.bfloat16)

    def loop(body):
        lax.fori_loop(0, groups, lambda g, carry: (body(g), carry)[1], 0)

    tok_copy.wait()
    for p in range(4):
        h, kk = p // 2, p % 2
        tq[z * 4 + p] = quantize(tokf[pl.ds(h * half, half), pl.ds(kk * dk, dk)], own_scale)
        if p == 0:
            pl.semaphore_wait(barrier, 2 + (z > 0).astype(jnp.int32) + (z < 3).astype(jnp.int32))

        @pl.when(z > 0)
        def _():
            z_copy(z, p, False).start()

        @pl.when(z < 3)
        def _():
            z_copy(z, p, True).start()

    step_rows = 256
    own_descale = pick(table, z)

    def stream(g):
        total = jnp.zeros((rows, wide), jnp.float32)
        for kk in range(2):
            i = g * 2 + kk
            slot = i % nstage
            stage_copy(g, kk, slot).wait()

            def part(j, total):
                at = pl.ds(pl.multiple_of(j * step_rows, step_rows), step_rows)
                rounded = quantize(stage[slot, at, :], weight_scale)
                wq[g, pl.ds(pl.multiple_of(kk * dk + j * step_rows, step_rows), step_rows), :] = rounded
                lhs = jnp.concatenate([tq[z * 4 + kk, :, at], tq[z * 4 + 2 + kk, :, at]], axis=0)
                return total + jnp.dot(lhs, rounded, preferred_element_type=jnp.float32)

            total = lax.fori_loop(0, dk // step_rows, part, total)

            @pl.when(i + nstage < groups * 2)
            def _():
                later = i + nstage
                stage_copy_dyn(later, slot).start()
        total = total * own_descale
        for h in range(2):
            give(blocks[0], h, g, total[h * half:(h + 1) * half])

    def stage_copy_dyn(i, slot):
        return pltpu.make_async_copy(
            w_hbm.at[pl.ds(pl.multiple_of((i % 2) * dk, dk), dk),
                     pl.ds(pl.multiple_of((i // 2) * wide, wide), wide)],
            stage.at[slot], stage_sem.at[slot])

    def stream_step(g):
        stream(g)
        for p in range(4):
            @pl.when(g == p + 1)
            def _():
                forward(blocks[1], p)
                forward(blocks[2], p)
        for p in range(2):
            @pl.when(g == groups - 2 + p)
            def _():
                forward(blocks[3], p)

    loop(stream_step)
    for h in range(2):
        loop(lambda g: pair_sum(blocks[0], h, g))

    for b in blocks[1:3]:
        for p in range(4):
            arrive(b, p)
    scales = [pick(table, b) for b in blocks]

    def two(g):
        total = None
        for kk in range(2):
            lhs = jnp.concatenate([tq[b * 4 + h * 2 + kk] for b in blocks[1:3] for h in range(2)], axis=0)
            term = jnp.dot(lhs, wq[g, pl.ds(kk * dk, dk), :], preferred_element_type=jnp.float32)
            total = term if total is None else total + term
        for i in range(4):
            k, h = 1 + i // 2, i % 2
            give(blocks[k], h, g, total[i * half:(i + 1) * half] * scales[k])

    loop(two)
    forward(blocks[3], 2)
    forward(blocks[3], 3)
    for k in (1, 2):
        for h in range(2):
            loop(lambda g: pair_sum(blocks[k], h, g))

    last = blocks[3]
    for h in range(2):
        arrive(last, h * 2)

        def first(g):
            accb[g] = jnp.dot(tq[last * 4 + h * 2], wq[g, pl.ds(0, dk), :], preferred_element_type=jnp.float32)

        loop(first)
        arrive(last, h * 2 + 1)

        def second(g):
            total = accb[g] + jnp.dot(tq[last * 4 + h * 2 + 1], wq[g, pl.ds(dk, dk), :],
                                      preferred_element_type=jnp.float32)
            give(last, h, g, total * scales[3])

            @pl.when(g > 0)
            def _():
                pair_sum(last, h, g - 1)

        loop(second)
        pair_sum(last, h, groups - 1)
    for h in range(2):
        loop(lambda g: final_sum(h, g))

    for p in range(4):
        @pl.when(z > 0)
        def _():
            z_copy(z, p, False).wait_send()

        @pl.when(z < 3)
        def _():
            z_copy(z, p, True).wait_send()

        @pl.when(middle)
        def _():
            for k in range(1, 4):
                hop(blocks[k], p, lambda copy: copy.wait_send())
    for h in range(2):
        def sent(g):
            p_copy(0, h, g).wait_send()
            p_copy(1, h, g).wait_send()
            x_copy(h, g).wait_send()

        loop(sent)


def fused_call(tokens, weight, token_amax, token_window, weight_amax, weight_window):
    rows, depth = tokens.shape
    columns = weight.shape[1]
    wide, nstage = columns // 8, 3
    groups, half, dk = 8, rows // 2, depth // 2
    dma = pltpu.SemaphoreType.DMA
    bf16, f32 = jnp.bfloat16, jnp.float32
    vmem, hbm = pl.BlockSpec(memory_space=pltpu.VMEM), pl.BlockSpec(memory_space=pl.ANY)
    return pl.pallas_call(
        functools.partial(fused, (rows, depth, wide, nstage)),
        out_shape=jax.ShapeDtypeStruct((rows, columns), bf16),
        in_specs=[hbm, hbm, vmem, vmem, vmem, vmem],
        out_specs=vmem,
        scratch_shapes=[
            pltpu.VMEM((rows, depth), f32),
            pltpu.VMEM((nstage, dk, wide), f32),
            pltpu.VMEM((groups, depth, wide), bf16),
            pltpu.VMEM((16, half, dk), bf16),
            pltpu.VMEM((4 * groups, half, wide), f32),
            pltpu.VMEM((4 * groups, half, wide), bf16),
            pltpu.VMEM((4 * groups, half, wide), bf16),
            pltpu.VMEM((2 * groups, half, wide), bf16),
            pltpu.VMEM((2 * groups, half, wide), bf16),
            pltpu.VMEM((groups, half, wide), f32),
            dma, dma((nstage,)),
            dma((32,)), dma((16,)),
            dma((4 * groups,)), dma((4 * groups,)),
            dma((2 * groups,)), dma((2 * groups,)),
        ],
        compiler_params=pltpu.CompilerParams(
            collective_id=0, has_side_effects=True, vmem_limit_bytes=58 * MIB),
        cost_estimate=pl.CostEstimate(
            flops=2 * 4 * rows * depth * columns, bytes_accessed=4 * depth * columns, transcendentals=0),
        name="project",
    )(tokens, weight, token_amax, token_window, weight_amax, weight_window)


def solution(mesh):
    def shards(tokens, weight, *scales):
        rows, depth = tokens.shape
        columns = weight.shape[1]
        fits = 2 * depth * columns <= 32 * MIB and rows == TOK_DEV
        tiles = depth % 1024 == 0 and columns % 1024 == 0
        if mesh.shape["col"] == 4 and mesh.shape["row"] == 4 and fits and tiles:
            return fused_call(tokens, weight, *scales)
        return general(tokens, weight, *scales)

    return jax.shard_map(
        shards,
        mesh=mesh,
        in_specs=(
            P(("groups", "col"), "row"),
            P("row", "col"),
            P("groups", "row", None),
            P("groups", "row"),
            P("row", "col", None),
            P("row", "col"),
        ),
        out_specs=P(("groups", "row"), "col"),
        check_vma=False,
    )
```

```python
import functools

import jax
import jax.numpy as jnp
from jax import lax
from jax.experimental import pallas as pl
from jax.experimental.pallas import tpu as pltpu
from jax.sharding import PartitionSpec as P

TOK_DEV = 64
QMAX = 448.0
MESH = pl.DeviceIdType.MESH
MIB = 1 << 20


def delayed_scale(history, window):
    hlen = history.shape[-1]
    position = jnp.arange(hlen, dtype=jnp.int32)
    keep = position >= (hlen - window)[..., None]
    amax = jnp.max(jnp.where(keep, history, jnp.float32(0.0)), axis=-1)
    return QMAX / amax


def quantize(values, scale):
    return jnp.clip(values * scale, -QMAX, QMAX).astype(jnp.bfloat16)


def row_descale(table, count):
    block_of = jnp.arange(count, dtype=jnp.int32) // TOK_DEV
    owners = jnp.arange(table.shape[0], dtype=jnp.int32)
    onehot = block_of[:, None] == owners[None, :]
    return jnp.sum(jnp.where(onehot, table[None, :], jnp.float32(0.0)), axis=1)


def general(tokens, weight, token_amax, token_window, weight_amax, weight_window):
    token_scale = delayed_scale(token_amax[:, 0, :], token_window[:, 0])
    own_scale = lax.dynamic_index_in_dim(token_scale, lax.axis_index("col"), 0, keepdims=False)
    tile_scale = delayed_scale(weight_amax[0, 0, :], weight_window[0, 0])
    token_q = quantize(tokens, own_scale)
    weight_q = quantize(weight, tile_scale)
    table = 1.0 / (token_scale * tile_scale)
    piece = lax.all_gather(token_q, "col", axis=0, tiled=True)
    values = jnp.dot(piece, weight_q, preferred_element_type=jnp.float32)
    partial_sum = values * row_descale(table, piece.shape[0])[:, None]
    summed = lax.psum_scatter(partial_sum, "row", scatter_dimension=0, tiled=True)
    return summed.astype(jnp.bfloat16)


def window_scale(history, window):
    position = lax.broadcasted_iota(jnp.int32, history.shape, 1)
    keep = position >= history.shape[1] - window
    return QMAX / jnp.max(jnp.where(keep, history, 0.0), axis=1, keepdims=True)


def fused(dims, tok_hbm, w_hbm, tam, twin, wam, wwin, out,
          tokf, stage, wq, tq, mine, psend, prec, xsend, xrec, accb,
          tok_sem, stage_sem, zs, zr, ps, pr, xs, xr):
    rows, depth, wide, nstage = dims
    dk, dq = depth // 2, depth // 4
    groups = wq.shape[0]
    z, r = lax.axis_index("col"), lax.axis_index("row")
    x, c = r // 2, r % 2
    sibling, across = x * 2 + (1 - c), (1 - x) * 2 + c
    middle = (z % 3) != 0

    low = z < 2
    zz = jnp.where(low, z, 3 - z)

    def order(k):
        b = (k + zz) % 2 if k < 2 else k
        return jnp.where(low, b, 3 - b)

    blocks = [order(k) for k in range(4)]

    def stage_copy(g, kk, slot):
        return pltpu.make_async_copy(
            w_hbm.at[pl.ds(pl.multiple_of(kk * dk, dk), dk), pl.ds(pl.multiple_of(g * wide, wide), wide)],
            stage.at[slot], stage_sem.at[slot])

    tok_copy = pltpu.make_async_copy(tok_hbm, tokf, tok_sem)
    tok_copy.start()
    barrier = pltpu.get_barrier_semaphore()
    for who in (sibling, across):
        pl.semaphore_signal(barrier, inc=1, device_id={"row": who}, device_id_type=MESH)

    @pl.when(z > 0)
    def _():
        pl.semaphore_signal(barrier, inc=1, device_id={"col": z - 1}, device_id_type=MESH)

    @pl.when(z < 3)
    def _():
        pl.semaphore_signal(barrier, inc=1, device_id={"col": z + 1}, device_id_type=MESH)

    n_blocks = twin.shape[1]
    square = (n_blocks, n_blocks)
    diagonal = lax.broadcasted_iota(jnp.int32, square, 0) == lax.broadcasted_iota(jnp.int32, square, 1)
    windows = jnp.sum(jnp.where(diagonal, jnp.broadcast_to(twin[...], square), 0), axis=1, keepdims=True)
    token_scale = window_scale(tam[:, 0, :], windows)
    weight_scale = window_scale(wam[0], wwin[...])
    table = 1.0 / (token_scale * weight_scale)
    which = lax.broadcasted_iota(jnp.int32, table.shape, 0)

    def pick(values, b):
        return jnp.sum(jnp.where(which == b, values, 0.0), axis=0, keepdims=True)

    own_scale = pick(token_scale, z)

    def z_copy(b, p, right):
        to = z + 1 if right else z - 1
        piece = b * 4 + p
        return pltpu.make_async_remote_copy(
            src_ref=tq.at[piece], dst_ref=tq.at[piece],
            send_sem=zs.at[int(right) * 16 + piece], recv_sem=zr.at[piece],
            device_id={"col": to}, device_id_type=MESH)

    def hop(b, p, act):
        @pl.when(b > z)
        def _():
            act(z_copy(b, p, False))

        @pl.when(b < z)
        def _():
            act(z_copy(b, p, True))

    def own(p, act):
        @pl.when(z > 0)
        def _():
            act(z_copy(z, p, False))

        @pl.when(z < 3)
        def _():
            act(z_copy(z, p, True))

    def begin(copy):
        copy.start()

    def left(copy):
        copy.wait_send()

    def send(n):
        if 2 <= n < 6:
            own(n - 2, left)
        if n < 4:
            own(n, begin)
        else:
            @pl.when(middle)
            def _():
                for k in (1, 2) if n < 8 else (3,):
                    z_copy(blocks[k], n % 4, True).wait_recv()
                for k in () if n < 6 else (1, 2) if n < 10 else (3,):
                    hop(blocks[k], (n - 2) % 4, left)
                for k in (1, 2) if n < 8 else (3,):
                    hop(blocks[k], n % 4, begin)

    def arrive(b, p):
        @pl.when(jnp.logical_not(middle))
        def _():
            z_copy(b, p, True).wait_recv()

    def p_copy(slot, g):
        unit = slot * groups + g
        return pltpu.make_async_remote_copy(
            src_ref=psend.at[unit], dst_ref=prec.at[unit],
            send_sem=ps.at[unit], recv_sem=pr.at[unit],
            device_id={"row": sibling}, device_id_type=MESH)

    def x_copy(g):
        return pltpu.make_async_remote_copy(
            src_ref=xsend.at[g], dst_ref=xrec.at[g],
            send_sem=xs.at[g], recv_sem=xr.at[g],
            device_id={"row": across}, device_id_type=MESH)

    def give(b, g, values):
        slot = (b // 2 + x) % 2
        unit = slot * groups + g

        @pl.when(b % 2 != c)
        def _():
            psend[unit] = values.astype(jnp.bfloat16)
            p_copy(slot, g).start()

        @pl.when(b % 2 == c)
        def _():
            mine[unit] = values

    def pair_sum(b, g):
        slot = (b // 2 + x) % 2
        unit = slot * groups + g

        @pl.when(b % 2 == c)
        def _():
            p_copy(slot, g).wait_recv()
            total = mine[unit] + prec[unit].astype(jnp.float32)

            @pl.when(slot == 1)
            def _():
                xsend[g] = total.astype(jnp.bfloat16)
                x_copy(g).start()

            @pl.when(slot == 0)
            def _():
                mine[unit] = total

    def final_sum(g):
        x_copy(g).wait_recv()
        total = mine[g] + xrec[g].astype(jnp.float32)
        out[:, pl.ds(pl.multiple_of(g * wide, wide), wide)] = total.astype(jnp.bfloat16)

    def loop(body):
        lax.fori_loop(0, groups, lambda g, carry: (body(g), carry)[1], 0)

    tok_copy.wait()
    for p in range(4):
        tq[z * 4 + p] = quantize(tokf[:, pl.ds(p * dq, dq)], own_scale)
        if p == 0:
            pl.semaphore_wait(barrier, 2 + (z > 0).astype(jnp.int32) + (z < 3).astype(jnp.int32))

        if p < 2:
            send(p)

    for i in range(nstage):
        stage_copy(i // 2, i % 2, i).start()
    step_rows = 512

    def stream_step(g):
        for kk in range(2):
            i = g * 2 + kk
            slot = i % nstage
            stage_copy(g, kk, slot).wait()

            def part(j, carry):
                at = pl.multiple_of(j * step_rows, step_rows)
                wq[g, pl.ds(pl.multiple_of(kk * dk + at, step_rows), step_rows), :] = quantize(
                    stage[slot, pl.ds(at, step_rows), :], weight_scale)
                return carry

            lax.fori_loop(0, dk // step_rows, part, 0)

            @pl.when(i + nstage < groups * 2)
            def _():
                stage_copy((i + nstage) // 2, (i + nstage) % 2, slot).start()
        for n in range(2, 8):
            @pl.when(g == n - 1)
            def _():
                send(n)

    loop(stream_step)
    scales = [pick(table, b) for b in blocks]

    def term(bs, q, g):
        lhs = jnp.concatenate([tq[b * 4 + q] for b in bs], axis=0)
        return jnp.dot(lhs, wq[g, pl.ds(q * dq, dq), :], preferred_element_type=jnp.float32)

    for p in range(4):
        arrive(blocks[1], p)

    def two(g):
        total = term(blocks[:2], 0, g)
        for q in range(1, 4):
            total += term(blocks[:2], q, g)
        for k in range(2):
            give(blocks[k], g, total[k * rows:(k + 1) * rows] * scales[k])
        for n in (8, 9):
            @pl.when(g == (n - 8) * 4 + 2)
            def _():
                send(n)

    loop(two)
    for k in range(2):
        loop(lambda g: pair_sum(blocks[k], g))

    for k in (2, 3):
        for q in range(4):
            if k == 2 and q < 2:
                send(10 + q)
            arrive(blocks[k], q)
            some = 4 if q < 3 else 2

            def quarter(n, carry):
                units = [n * some + i for i in range(some)]
                totals = [term(blocks[k:k + 1], q, g) for g in units]
                if q > 0:
                    totals = [accb[g] + total for g, total in zip(units, totals)]
                for g, total in zip(units, totals):
                    if q < 3:
                        accb[g] = total
                    else:
                        give(blocks[k], g, total * scales[k])
                if q == 3:
                    @pl.when(n > 0)
                    def _():
                        for g in units:
                            pair_sum(blocks[k], g - some)
                return carry

            lax.fori_loop(0, groups // some, quarter, 0)
        for i in range(2):
            pair_sum(blocks[k], groups - 2 + i)
    loop(final_sum)

    @pl.when(middle)
    def _():
        for p in (2, 3):
            hop(blocks[3], p, left)

    def sent(g):
        p_copy(0, g).wait_send()
        p_copy(1, g).wait_send()
        x_copy(g).wait_send()

    loop(sent)


def fused_call(tokens, weight, token_amax, token_window, weight_amax, weight_window):
    rows, depth = tokens.shape
    columns = weight.shape[1]
    wide, nstage = columns // 8, 3
    groups, dk = 8, depth // 2
    dma = pltpu.SemaphoreType.DMA
    bf16, f32 = jnp.bfloat16, jnp.float32
    vmem, hbm = pl.BlockSpec(memory_space=pltpu.VMEM), pl.BlockSpec(memory_space=pl.ANY)
    return pl.pallas_call(
        functools.partial(fused, (rows, depth, wide, nstage)),
        out_shape=jax.ShapeDtypeStruct((rows, columns), bf16),
        in_specs=[hbm, hbm, vmem, vmem, vmem, vmem],
        out_specs=vmem,
        scratch_shapes=[
            pltpu.VMEM((rows, depth), f32),
            pltpu.VMEM((nstage, dk, wide), f32),
            pltpu.VMEM((groups, depth, wide), bf16),
            pltpu.VMEM((16, rows, depth // 4), bf16),
            pltpu.VMEM((2 * groups, rows, wide), f32),
            pltpu.VMEM((2 * groups, rows, wide), bf16),
            pltpu.VMEM((2 * groups, rows, wide), bf16),
            pltpu.VMEM((groups, rows, wide), bf16),
            pltpu.VMEM((groups, rows, wide), bf16),
            pltpu.VMEM((groups, rows, wide), f32),
            dma, dma((nstage,)),
            dma((32,)), dma((16,)),
            dma((2 * groups,)), dma((2 * groups,)),
            dma((groups,)), dma((groups,)),
        ],
        compiler_params=pltpu.CompilerParams(
            collective_id=0, has_side_effects=True, vmem_limit_bytes=58 * MIB),
        cost_estimate=pl.CostEstimate(
            flops=2 * 4 * rows * depth * columns, bytes_accessed=4 * depth * columns, transcendentals=0),
        name="project",
    )(tokens, weight, token_amax, token_window.T, weight_amax, weight_window)


def solution(mesh):
    def shards(tokens, weight, *scales):
        rows, depth = tokens.shape
        columns = weight.shape[1]
        fits = 2 * depth * columns <= 32 * MIB and rows == TOK_DEV
        tiles = depth % 1024 == 0 and columns % 1024 == 0
        if mesh.shape["col"] == 4 and mesh.shape["row"] == 4 and fits and tiles:
            return fused_call(tokens, weight, *scales)
        return general(tokens, weight, *scales)

    return jax.shard_map(
        shards,
        mesh=mesh,
        in_specs=(
            P(("groups", "col"), "row"),
            P("row", "col"),
            P("groups", "row", None),
            P("groups", "row"),
            P("row", "col", None),
            P("row", "col"),
        ),
        out_specs=P(("groups", "row"), "col"),
        check_vma=False,
    )
```

```python
import functools

import jax
import jax.numpy as jnp
from jax import lax
from jax.experimental import pallas as pl
from jax.experimental.pallas import tpu as pltpu
from jax.sharding import PartitionSpec as P

TOK_DEV = 64
QMAX = 448.0
MESH = pl.DeviceIdType.MESH
MIB = 1 << 20


def delayed_scale(history, window):
    hlen = history.shape[-1]
    position = jnp.arange(hlen, dtype=jnp.int32)
    keep = position >= (hlen - window)[..., None]
    amax = jnp.max(jnp.where(keep, history, jnp.float32(0.0)), axis=-1)
    return QMAX / amax


def quantize(values, scale):
    return jnp.clip(values * scale, -QMAX, QMAX).astype(jnp.bfloat16)


def row_descale(table, count):
    block_of = jnp.arange(count, dtype=jnp.int32) // TOK_DEV
    owners = jnp.arange(table.shape[0], dtype=jnp.int32)
    onehot = block_of[:, None] == owners[None, :]
    return jnp.sum(jnp.where(onehot, table[None, :], jnp.float32(0.0)), axis=1)


def general(tokens, weight, token_amax, token_window, weight_amax, weight_window):
    token_scale = delayed_scale(token_amax[:, 0, :], token_window[:, 0])
    own_scale = lax.dynamic_index_in_dim(token_scale, lax.axis_index("col"), 0, keepdims=False)
    tile_scale = delayed_scale(weight_amax[0, 0, :], weight_window[0, 0])
    token_q = quantize(tokens, own_scale)
    weight_q = quantize(weight, tile_scale)
    table = 1.0 / (token_scale * tile_scale)
    piece = lax.all_gather(token_q, "col", axis=0, tiled=True)
    values = jnp.dot(piece, weight_q, preferred_element_type=jnp.float32)
    partial_sum = values * row_descale(table, piece.shape[0])[:, None]
    summed = lax.psum_scatter(partial_sum, "row", scatter_dimension=0, tiled=True)
    return summed.astype(jnp.bfloat16)


def window_scale(history, window):
    position = lax.broadcasted_iota(jnp.int32, history.shape, 1)
    keep = position >= history.shape[1] - window
    return QMAX / jnp.max(jnp.where(keep, history, 0.0), axis=1, keepdims=True)


def fused(dims, tok_hbm, w_hbm, tam, twin, wam, wwin, out,
          tokf, stage, wq, tq, mine, psend, prec, xsend, xrec, accb,
          tok_sem, stage_sem, zs, zr, ps, pr, xs, xr):
    rows, depth, wide, nstage = dims
    dk, dq = depth // 2, depth // 4
    groups = wq.shape[0]
    z, r = lax.axis_index("col"), lax.axis_index("row")
    x, c = r // 2, r % 2
    sibling, across = x * 2 + (1 - c), (1 - x) * 2 + c
    middle = (z % 3) != 0

    low = z < 2
    zz = jnp.where(low, z, 3 - z)

    def order(k):
        b = (k + zz) % 2 if k < 2 else k
        return jnp.where(low, b, 3 - b)

    blocks = [order(k) for k in range(4)]

    def stage_copy(g, kk, slot):
        return pltpu.make_async_copy(
            w_hbm.at[pl.ds(pl.multiple_of(kk * dk, dk), dk), pl.ds(pl.multiple_of(g * wide, wide), wide)],
            stage.at[slot], stage_sem.at[slot])

    tok_copy = pltpu.make_async_copy(tok_hbm, tokf, tok_sem)
    tok_copy.start()
    barrier = pltpu.get_barrier_semaphore()
    for who in (sibling, across):
        pl.semaphore_signal(barrier, inc=1, device_id={"row": who}, device_id_type=MESH)

    @pl.when(z > 0)
    def _():
        pl.semaphore_signal(barrier, inc=1, device_id={"col": z - 1}, device_id_type=MESH)

    @pl.when(z < 3)
    def _():
        pl.semaphore_signal(barrier, inc=1, device_id={"col": z + 1}, device_id_type=MESH)

    n_blocks = twin.shape[1]
    square = (n_blocks, n_blocks)
    diagonal = lax.broadcasted_iota(jnp.int32, square, 0) == lax.broadcasted_iota(jnp.int32, square, 1)
    windows = jnp.sum(jnp.where(diagonal, jnp.broadcast_to(twin[...], square), 0), axis=1, keepdims=True)
    token_scale = window_scale(tam[:, 0, :], windows)
    weight_scale = window_scale(wam[0], wwin[...])
    table = 1.0 / (token_scale * weight_scale)
    which = lax.broadcasted_iota(jnp.int32, table.shape, 0)

    def pick(values, b):
        return jnp.sum(jnp.where(which == b, values, 0.0), axis=0, keepdims=True)

    own_scale = pick(token_scale, z)

    def z_copy(b, p, right):
        to = z + 1 if right else z - 1
        piece = b * 4 + p
        return pltpu.make_async_remote_copy(
            src_ref=tq.at[piece], dst_ref=tq.at[piece],
            send_sem=zs.at[int(right) * 16 + piece], recv_sem=zr.at[piece],
            device_id={"col": to}, device_id_type=MESH)

    def hop(b, p, act):
        @pl.when(b > z)
        def _():
            act(z_copy(b, p, False))

        @pl.when(b < z)
        def _():
            act(z_copy(b, p, True))

    def own(p, act):
        @pl.when(z > 0)
        def _():
            act(z_copy(z, p, False))

        @pl.when(z < 3)
        def _():
            act(z_copy(z, p, True))

    def begin(copy):
        copy.start()

    def left(copy):
        copy.wait_send()

    def send(n):
        if 2 <= n < 6:
            own(n - 2, left)
        if n < 4:
            own(n, begin)
        else:
            @pl.when(middle)
            def _():
                for k in (1, 2) if n < 8 else (3,):
                    z_copy(blocks[k], n % 4, True).wait_recv()
                for k in () if n < 6 else (1, 2) if n < 10 else (3,):
                    hop(blocks[k], (n - 2) % 4, left)
                for k in (1, 2) if n < 8 else (3,):
                    hop(blocks[k], n % 4, begin)

    def arrive(b, p):
        @pl.when(jnp.logical_not(middle))
        def _():
            z_copy(b, p, True).wait_recv()

    def p_copy(slot, g):
        unit = slot * groups + g
        return pltpu.make_async_remote_copy(
            src_ref=psend.at[unit], dst_ref=prec.at[unit],
            send_sem=ps.at[unit], recv_sem=pr.at[unit],
            device_id={"row": sibling}, device_id_type=MESH)

    def x_copy(g):
        return pltpu.make_async_remote_copy(
            src_ref=xsend.at[g], dst_ref=xrec.at[g],
            send_sem=xs.at[g], recv_sem=xr.at[g],
            device_id={"row": across}, device_id_type=MESH)

    def give(b, g, values):
        slot = (b // 2 + x) % 2
        unit = slot * groups + g

        @pl.when(b % 2 != c)
        def _():
            psend[unit] = values.astype(jnp.bfloat16)
            p_copy(slot, g).start()

        @pl.when(b % 2 == c)
        def _():
            mine[unit] = values

    def pair_sum(b, g):
        slot = (b // 2 + x) % 2
        unit = slot * groups + g

        @pl.when(b % 2 == c)
        def _():
            p_copy(slot, g).wait_recv()
            total = mine[unit] + prec[unit].astype(jnp.float32)

            @pl.when(slot == 1)
            def _():
                xsend[g] = total.astype(jnp.bfloat16)
                x_copy(g).start()

            @pl.when(slot == 0)
            def _():
                mine[unit] = total

    def final_sum(g):
        x_copy(g).wait_recv()
        total = mine[g] + xrec[g].astype(jnp.float32)
        out[:, pl.ds(pl.multiple_of(g * wide, wide), wide)] = total.astype(jnp.bfloat16)

    def loop(body):
        lax.fori_loop(0, groups, lambda g, carry: (body(g), carry)[1], 0)

    tok_copy.wait()
    for p in range(4):
        tq[z * 4 + p] = quantize(tokf[:, pl.ds(p * dq, dq)], own_scale)
        if p == 0:
            pl.semaphore_wait(barrier, 2 + (z > 0).astype(jnp.int32) + (z < 3).astype(jnp.int32))

        if p < 2:
            send(p)

    for i in range(nstage):
        stage_copy(i // 2, i % 2, i).start()
    step_rows = 512

    def stream_step(g):
        for kk in range(2):
            i = g * 2 + kk
            slot = i % nstage
            stage_copy(g, kk, slot).wait()

            def part(j, carry):
                at = pl.multiple_of(j * step_rows, step_rows)
                wq[g, pl.ds(pl.multiple_of(kk * dk + at, step_rows), step_rows), :] = quantize(
                    stage[slot, pl.ds(at, step_rows), :], weight_scale)
                return carry

            lax.fori_loop(0, dk // step_rows, part, 0)

            @pl.when(i + nstage < groups * 2)
            def _():
                stage_copy((i + nstage) // 2, (i + nstage) % 2, slot).start()
        for n in range(2, 8):
            @pl.when(g == n - 1)
            def _():
                send(n)

    loop(stream_step)
    scales = [pick(table, b) for b in blocks]

    def term(bs, q, g):
        lhs = jnp.concatenate([tq[b * 4 + q] for b in bs], axis=0)
        return jnp.dot(lhs, wq[g, pl.ds(q * dq, dq), :], preferred_element_type=jnp.float32)

    for p in range(4):
        arrive(blocks[1], p)

    def two(g):
        total = term(blocks[:2], 0, g)
        for q in range(1, 4):
            total += term(blocks[:2], q, g)
        for k in range(2):
            give(blocks[k], g, total[k * rows:(k + 1) * rows] * scales[k])
        for n in (8, 9):
            @pl.when(g == (n - 8) * 4 + 2)
            def _():
                send(n)

    loop(two)
    for k in range(2):
        loop(lambda g: pair_sum(blocks[k], g))

    for k, parts in ((2, ((0, 1), (2, 3))), (3, ((0, 1), (2,), (3,)))):
        for index, part in enumerate(parts):
            if k == 2:
                send(10 + index)
            for q in part:
                arrive(blocks[k], q)
            ends = part[-1] == 3
            some = 2 if ends else 4 // len(part)

            def portion(n, carry):
                units = [n * some + i for i in range(some)]
                totals = []
                for g in units:
                    total = term(blocks[k:k + 1], part[0], g)
                    for q in part[1:]:
                        total += term(blocks[k:k + 1], q, g)
                    totals.append(total)
                if index > 0:
                    totals = [accb[g] + total for g, total in zip(units, totals)]
                for g, total in zip(units, totals):
                    if ends:
                        give(blocks[k], g, total * scales[k])
                    else:
                        accb[g] = total
                if ends:
                    @pl.when(n > 0)
                    def _():
                        for g in units:
                            pair_sum(blocks[k], g - some)
                return carry

            lax.fori_loop(0, groups // some, portion, 0)
        for i in range(2):
            pair_sum(blocks[k], groups - 2 + i)

    loop(final_sum)

    @pl.when(middle)
    def _():
        for p in (2, 3):
            hop(blocks[3], p, left)

    def sent(g):
        p_copy(0, g).wait_send()
        p_copy(1, g).wait_send()
        x_copy(g).wait_send()

    loop(sent)


def fused_call(tokens, weight, token_amax, token_window, weight_amax, weight_window):
    rows, depth = tokens.shape
    columns = weight.shape[1]
    wide, nstage = columns // 8, 3
    groups, dk = 8, depth // 2
    dma = pltpu.SemaphoreType.DMA
    bf16, f32 = jnp.bfloat16, jnp.float32
    vmem, hbm = pl.BlockSpec(memory_space=pltpu.VMEM), pl.BlockSpec(memory_space=pl.ANY)
    return pl.pallas_call(
        functools.partial(fused, (rows, depth, wide, nstage)),
        out_shape=jax.ShapeDtypeStruct((rows, columns), bf16),
        in_specs=[hbm, hbm, vmem, vmem, vmem, vmem],
        out_specs=vmem,
        scratch_shapes=[
            pltpu.VMEM((rows, depth), f32),
            pltpu.VMEM((nstage, dk, wide), f32),
            pltpu.VMEM((groups, depth, wide), bf16),
            pltpu.VMEM((16, rows, depth // 4), bf16),
            pltpu.VMEM((2 * groups, rows, wide), f32),
            pltpu.VMEM((2 * groups, rows, wide), bf16),
            pltpu.VMEM((2 * groups, rows, wide), bf16),
            pltpu.VMEM((groups, rows, wide), bf16),
            pltpu.VMEM((groups, rows, wide), bf16),
            pltpu.VMEM((groups, rows, wide), f32),
            dma, dma((nstage,)),
            dma((32,)), dma((16,)),
            dma((2 * groups,)), dma((2 * groups,)),
            dma((groups,)), dma((groups,)),
        ],
        compiler_params=pltpu.CompilerParams(
            collective_id=0, has_side_effects=True, vmem_limit_bytes=58 * MIB),
        cost_estimate=pl.CostEstimate(
            flops=2 * 4 * rows * depth * columns, bytes_accessed=4 * depth * columns, transcendentals=0),
        name="project",
    )(tokens, weight, token_amax, token_window.T, weight_amax, weight_window)


def solution(mesh):
    def shards(tokens, weight, *scales):
        rows, depth = tokens.shape
        columns = weight.shape[1]
        fits = 2 * depth * columns <= 32 * MIB and rows == TOK_DEV
        tiles = depth % 1024 == 0 and columns % 1024 == 0
        if mesh.shape["col"] == 4 and mesh.shape["row"] == 4 and fits and tiles:
            return fused_call(tokens, weight, *scales)
        return general(tokens, weight, *scales)

    return jax.shard_map(
        shards,
        mesh=mesh,
        in_specs=(
            P(("groups", "col"), "row"),
            P("row", "col"),
            P("groups", "row", None),
            P("groups", "row"),
            P("row", "col", None),
            P("row", "col"),
        ),
        out_specs=P(("groups", "row"), "col"),
        check_vma=False,
    )
```
